32 devices in a mesh: gx: 8 (over z, core), gy: 4 (over y, x).
Axes of the slice: x: 2, y: 2, z: 4, core: 2. Of those that a mesh axis runs over, the one named last changes fastest.
Arguments:
- patches: bfloat16 [512, 6144], P('gy', 'gx'), may hold values from -40 to 40
- ln_gain: float32 [6144], P('gx'), may hold values from 0.5 to 1.5
- weight_in: bfloat16 [6144, 24576], P('gx', 'gy'), may hold values from -0.12757759 to 0.12757759
- weight_out: bfloat16 [24576, 6144], P('gy', 'gx'), may hold values from -0.063788795 to 0.063788795
- upstream: bfloat16 [512, 6144], P('gy', 'gx'), may hold values from -18 to 18
- row_in: float32 [6144], P('gx'), may hold values from 7.68 to 92.16
- col_in: float32 [24576], P('gy'), may hold values from 7.68 to 92.16
- row_out: float32 [24576], P('gy'), may hold values from 7.68 to 92.16
- col_out: float32 [6144], P('gx'), may hold values from 7.68 to 92.16
Outputs:
- output: bfloat16 [512, 6144], P('gy', 'gx')
- input_grad: float32 [512, 6144], P('gy', 'gx')
- update_in: float32 [6144, 24576], P('gx', 'gy')
- update_out: float32 [24576, 6144], P('gy', 'gx')
The draws below stay inside these ranges and needn't reach their ends.
All inputs are finite; a program needn't handle non-finite values.
Results may differ from the reference program's by a relative error of at most 0.028.
Values may be sent and summed in bfloat16 or wider, within the bound.
No kernel may reach another device: no remote copies, remote signals or barrier semaphores. Data moves between devices by JAX's collectives and lax.ppermute only.
A program may use at most 128 MiB of HBM per device.

```python
import math
import jax
import jax.numpy as jnp
from jax import lax

D = 6144
FF = 24576
ROWS = 512
N_GX = 8
N_GY = 4


def field_base(key, rows, cols):
    keys = jax.random.split(key, 1)
    base = jnp.clip(jax.random.normal(keys[0], (rows, cols), jnp.float32), -4.0, 4.0)
    return base


def scaled_field(key, rows, cols, row_low, row_high, noise_high):
    keys = jax.random.split(key, 3)
    base = field_base(keys[0], rows, cols)
    row_scale = jnp.exp(jax.random.uniform(keys[1], (rows, 1), jnp.float32, math.log(row_low), math.log(row_high)))
    rise = 3.0 ** (jnp.arange(cols, dtype=jnp.float32) / cols)
    noise = jnp.exp(jax.random.uniform(keys[2], (cols,), jnp.float32, 0.0, math.log(noise_high)))
    return base * row_scale * (rise * noise)[None, :]


def weight_field(key, rows, cols, fan_in, along_rows):
    keys = jax.random.split(key, 2)
    count = rows if along_rows else cols
    rise = 3.0 ** (jnp.arange(count, dtype=jnp.float32) / count - 0.5)
    noise = jnp.exp(jax.random.uniform(keys[1], (count,), jnp.float32, math.log(0.7), math.log(1.4)))
    factor = rise * noise / math.sqrt(fan_in)
    base = field_base(keys[0], rows, cols)
    if along_rows:
        return base * factor[:, None]
    return base * factor[None, :]


def rising_factor(key, count):
    noise = jnp.exp(jax.random.uniform(key, (count,), jnp.float32, math.log(0.5), math.log(2.0)))
    rise = 3.0 ** (jnp.arange(count, dtype=jnp.float32) / count)
    return ROWS * 0.03 * rise * noise


def draw_patches(key, part):
    return scaled_field(jax.random.fold_in(key, 11), ROWS, D, 0.1, 1.0, 3.3).astype(jnp.bfloat16)


def draw_upstream(key, part):
    return scaled_field(jax.random.fold_in(key, 12), ROWS, D, 0.3, 1.0, 1.5).astype(jnp.bfloat16)


def draw_weight_in(key, part):
    return weight_field(jax.random.fold_in(key, 13), D, FF, D, False).astype(jnp.bfloat16)


def draw_weight_out(key, part):
    return weight_field(jax.random.fold_in(key, 14), FF, D, FF, True).astype(jnp.bfloat16)


def draw_row_in(key, part):
    return rising_factor(jax.random.fold_in(key, 15), D)


def draw_col_in(key, part):
    return rising_factor(jax.random.fold_in(key, 16), FF)


def draw_row_out(key, part):
    return rising_factor(jax.random.fold_in(key, 17), FF)


def draw_col_out(key, part):
    return rising_factor(jax.random.fold_in(key, 18), D)


def setup_inputs(seed: int = 0) -> dict:
    seeds = jax.random.split(jax.random.key(seed), 10)
    return {
        "patches": draw_patches(jax.random.fold_in(seeds[9], 71), 0),
        "ln_gain": jnp.clip(1.0 + 0.1 * jax.random.normal(seeds[1], (D,), jnp.float32), 0.5, 1.5),
        "weight_in": draw_weight_in(jax.random.fold_in(seeds[9], 71), 0),
        "weight_out": draw_weight_out(jax.random.fold_in(seeds[9], 71), 0),
        "upstream": draw_upstream(jax.random.fold_in(seeds[9], 71), 0),
        "row_in": draw_row_in(jax.random.fold_in(seeds[9], 71), 0),
        "col_in": draw_col_in(jax.random.fold_in(seeds[9], 71), 0),
        "row_out": draw_row_out(jax.random.fold_in(seeds[9], 71), 0),
        "col_out": draw_col_out(jax.random.fold_in(seeds[9], 71), 0),
    }


def grouped_sum(left, right, groups, right_dim):
    rows = left.shape[0]
    width = left.shape[1] // groups
    lefts = left.reshape(rows, groups, width).transpose(1, 0, 2)
    if right_dim == 0:
        rights = right.reshape(groups, width, right.shape[1])
        dims = (((1,), (0,)), ((), ()))
        cols = right.shape[1]
    else:
        rights = right.reshape(right.shape[0], groups, width).transpose(1, 0, 2)
        dims = (((1,), (1,)), ((), ()))
        cols = right.shape[0]

    def accumulate(total, blocks):
        product = lax.dot_general(blocks[0], blocks[1], dims, preferred_element_type=jnp.float32)
        rounded = lax.optimization_barrier(product.astype(jnp.bfloat16))
        return (total + rounded.astype(jnp.float32), None)
    total, unused = lax.scan(accumulate, jnp.zeros((rows, cols), jnp.float32), (lefts, rights))
    return total

def rounded_once(values):
    return lax.optimization_barrier(values.astype(jnp.bfloat16)).astype(jnp.float32)

def factored(grad, row_prev, col_prev):
    squares = grad * grad + 1e-30
    row_new = 0.9 * row_prev + 0.1 * lax.optimization_barrier(jnp.mean(squares, axis=1))
    col_new = 0.9 * col_prev + 0.1 * lax.optimization_barrier(jnp.mean(squares, axis=0))
    scale = jnp.mean(row_new)
    return grad / jnp.sqrt(row_new[:, None] * col_new[None, :] / scale)

def reference(patches, ln_gain, weight_in, weight_out, upstream, row_in, col_in, row_out, col_out):
    x_float = patches.astype(jnp.float32)
    row_mean = lax.optimization_barrier(jnp.mean(x_float, axis=1, keepdims=True))
    row_var = lax.optimization_barrier(jnp.mean(x_float * x_float, axis=1, keepdims=True)) - row_mean * row_mean
    inv_std = lax.rsqrt(row_var + 1e-06)
    unit = (x_float - row_mean) * inv_std
    normed = (unit * ln_gain[None, :]).astype(jnp.bfloat16)
    hidden_pre = rounded_once(grouped_sum(normed, weight_in, N_GX, 0))
    phi = 0.5 * (1.0 + lax.erf(hidden_pre * 0.7071067811865476))
    hidden = (hidden_pre * phi).astype(jnp.bfloat16)
    branch = grouped_sum(hidden, weight_out, N_GY, 0)
    output = (x_float + branch).astype(jnp.bfloat16)
    hidden_grad = rounded_once(grouped_sum(upstream, weight_out, N_GX, 1))
    slope = phi + hidden_pre * jnp.exp(-0.5 * hidden_pre * hidden_pre) * 0.3989422804014327
    act_grad = (hidden_grad * slope).astype(jnp.bfloat16)
    grad_out = lax.dot_general(hidden, upstream, (((0,), (0,)), ((), ())), preferred_element_type=jnp.float32)
    grad_in = lax.dot_general(normed, act_grad, (((0,), (0,)), ((), ())), preferred_element_type=jnp.float32)
    normed_grad = grouped_sum(act_grad, weight_in, N_GY, 1)
    scaled = normed_grad * ln_gain[None, :]
    first_mean = lax.optimization_barrier(jnp.mean(scaled, axis=1, keepdims=True))
    second_mean = lax.optimization_barrier(jnp.mean(scaled * unit, axis=1, keepdims=True))
    input_grad = upstream.astype(jnp.float32) + inv_std * (scaled - first_mean - unit * second_mean)
    update_in = factored(grad_in, row_in, col_in)
    update_out = factored(grad_out, row_out, col_out)
    return (output, input_grad, update_in, update_out)
```

```python
import functools

import jax
import jax.numpy as jnp
from jax import lax
from jax.experimental import pallas as pl
from jax.experimental.pallas import tpu as pltpu
from jax.sharding import PartitionSpec as P

F32 = jnp.float32
BF16 = jnp.bfloat16
VMEM = 58 * 2**20
RUNS = (12,)


def block(total, limit):
    best = 128
    for width in range(128, min(total, limit) + 1, 128):
        if total % width == 0:
            best = width
    return best


def launch(kernel, grid, in_specs, out_specs, out_shape, args, after=(), carry=(), name="kernel"):
    many = isinstance(out_shape, list)
    shapes = out_shape if many else [out_shape]
    specs = out_specs if many else [out_specs]
    hidden = len(after) + len(carry)
    idle = [pl.BlockSpec(memory_space=pl.ANY)]

    def wrapped(*refs):
        inputs, rest = refs[: len(args)], refs[len(args) + hidden :]
        kernel(*inputs, *rest[: len(shapes)])

    results = pl.pallas_call(
        wrapped,
        grid=grid,
        in_specs=list(in_specs) + idle * hidden,
        out_specs=specs + idle * len(carry),
        out_shape=shapes + [jax.ShapeDtypeStruct(c.shape, c.dtype) for c in carry],
        input_output_aliases={len(args) + len(after) + n: len(shapes) + n for n in range(len(carry))},
        compiler_params=pltpu.CompilerParams(vmem_limit_bytes=VMEM),
        cost_estimate=pl.CostEstimate(flops=0, bytes_accessed=0, transcendentals=0),
        name=name,
    )(*args, *after, *carry)
    own = results[: len(shapes)]
    return (list(own) if many else own[0]), list(results[len(shapes) :])


def aligned(width, start, limit):
    step = block(width, limit)
    while start % step:
        step = block(width, step - 128)
    return step, start // step


def project(rows, weight, start, width, dim, after=(), carry=(), limit=1536):
    count, depth = rows.shape
    step, first = aligned(width, start, limit)

    def kernel(x, w, o):
        dims = (((1,), (dim,)), ((), ()))
        o[...] = lax.dot_general(x[...], w[...], dims, preferred_element_type=F32).astype(o.dtype)

    if dim == 0:
        spec = pl.BlockSpec((depth, step), lambda i: (0, first + i))
    else:
        spec = pl.BlockSpec((step, depth), lambda i: (first + i, 0))
    return launch(
        kernel,
        (width // step,),
        [pl.BlockSpec((count, depth), lambda i: (0, 0)), spec],
        pl.BlockSpec((count, step), lambda i: (0, i)),
        jax.ShapeDtypeStruct((count, width), BF16),
        (rows, weight),
        after,
        carry,
        name="project",
    )


def parts_specs(parts, which, step, index):
    blocks, _, rows, _ = parts[0].shape
    return [pl.BlockSpec((blocks, 1, rows, step), lambda i: (0, which, 0, index(i)))] * len(parts)


def whole_rows(refs):
    blocks, _, rows, step = refs[0].shape
    whole = [r[:, 0].reshape(blocks * rows, step) for r in refs]
    return whole[0] if len(whole) == 1 else jnp.concatenate(whole)


def consume(parts, which, left, weight, start, dim, before=None, after=(), carry=(), limit=1536):
    depth, count = left.shape
    width = parts[0].shape[3]
    step, first = aligned(width, start, limit)
    earlier = () if before is None else tuple(before)

    def kernel(x, w, *rest):
        prior, (cols, lanes, product) = rest[len(parts) : -3], rest[-3:]
        a = whole_rows(rest[: len(parts)])
        g = jnp.dot(x[...], a, preferred_element_type=F32)
        s = g * g
        cols[...] = jnp.sum(s, axis=0, keepdims=True)
        folded = s[:, :128]
        for j in range(1, step // 128):
            folded += s[:, j * 128 : (j + 1) * 128]
        part = lax.dot_general(a, w[...], (((1,), (dim,)), ((), ())), preferred_element_type=F32)

        @pl.when(pl.program_id(0) == 0)
        def _():
            lanes[...] = folded + prior[0][...] if prior else folded
            product[...] = part + prior[1][...] if prior else part

        @pl.when(pl.program_id(0) != 0)
        def _():
            lanes[...] += folded
            product[...] += part

    if dim == 0:
        spec = pl.BlockSpec((step, depth), lambda i: (first + i, 0))
    else:
        spec = pl.BlockSpec((depth, step), lambda i: (0, first + i))
    lane_spec = pl.BlockSpec((depth, 128), lambda i: (0, 0))
    product_spec = pl.BlockSpec((count, depth), lambda i: (0, 0))
    return launch(
        kernel,
        (width // step,),
        [pl.BlockSpec((depth, count), lambda i: (0, 0)), spec]
        + parts_specs(parts, which, step, lambda i: i)
        + ([lane_spec, product_spec] if earlier else []),
        [pl.BlockSpec((1, step), lambda i: (0, i)), lane_spec, product_spec],
        [
            jax.ShapeDtypeStruct((1, width), F32),
            jax.ShapeDtypeStruct((depth, 128), F32),
            jax.ShapeDtypeStruct((count, depth), F32),
        ],
        (left, weight, *parts, *earlier),
        after,
        carry,
        name="consume",
    )


def gelu(pre):
    phi = 0.5 * (1.0 + lax.erf(pre * 0.7071067811865476))
    slope = phi + pre * jnp.exp(-0.5 * pre * pre) * 0.3989422804014327
    return pre * phi, slope


def activate(pre, grad=None, after=(), carry=()):
    rows, width = pre.shape
    step = block(width, 1024)

    def kernel(p, *refs):
        value, slope = gelu(p[...].astype(F32))
        if grad is None:
            refs[0][0] = value.astype(BF16)
            refs[1][...] = slope
        else:
            refs[1][0] = value.astype(BF16)
            refs[1][1] = (refs[0][...].astype(F32) * slope).astype(BF16)

    spec = pl.BlockSpec((rows, step), lambda i: (0, i))
    kinds = 1 if grad is None else 2
    out_specs = [pl.BlockSpec((kinds, rows, step), lambda i: (0, 0, i))]
    out_shape = [jax.ShapeDtypeStruct((kinds, rows, width), BF16)]
    if grad is None:
        out_specs, out_shape = out_specs + [spec], out_shape + [jax.ShapeDtypeStruct((rows, width), F32)]
    return launch(
        kernel,
        (width // step,),
        [spec] if grad is None else [spec, spec],
        out_specs,
        out_shape,
        (pre,) if grad is None else (pre, grad),
        after,
        carry,
        name="activate",
    )


def write_update(side, pieces, row_scale, col_scale, hidden_rows, after=(), carry=(), limit=1024):
    widths = [parts[0].shape[3] for parts, _ in pieces]
    per = len(pieces[0][0])
    step = block(functools.reduce(gcd, widths), limit)
    counts = [w // step for w in widths]
    offsets = [sum(counts[:n]) for n in range(len(counts))]
    total = sum(widths)
    features = side.shape[1] if hidden_rows else side.shape[0]

    def kernel(*refs):
        x, acts, rows, cols, o = refs[0], refs[1 : 1 + per * len(pieces)], refs[-3], refs[-2], refs[-1]
        i = pl.program_id(0)
        for n, (first, blocks) in enumerate(zip(offsets, counts)):

            @pl.when(jnp.logical_and(i >= first, i < first + blocks))
            def _(n=n):
                a = whole_rows(acts[n * per : (n + 1) * per])
                if hidden_rows:
                    g = lax.dot_general(a, x[...], (((0,), (0,)), ((), ())), preferred_element_type=F32)
                    tall = jnp.transpose(jnp.broadcast_to(rows[...], (8, step)))[:, :1]
                    o[...] = g * tall * cols[...]
                else:
                    g = jnp.dot(x[...], a, preferred_element_type=F32)
                    o[...] = g * rows[...] * cols[...]

    def place(n):
        return lambda i: jnp.clip(i - offsets[n], 0, counts[n] - 1)

    if hidden_rows:
        scale_specs = [pl.BlockSpec((1, step), lambda i: (0, i)), pl.BlockSpec((1, features), lambda i: (0, 0))]
        out_spec = pl.BlockSpec((step, features), lambda i: (i, 0))
        shape = (total, features)
    else:
        scale_specs = [pl.BlockSpec((features, 1), lambda i: (0, 0)), pl.BlockSpec((1, step), lambda i: (0, i))]
        out_spec = pl.BlockSpec((features, step), lambda i: (0, i))
        shape = (features, total)
    piece_specs = [s for n, (parts, which) in enumerate(pieces) for s in parts_specs(parts, which, step, place(n))]
    return launch(
        kernel,
        (total // step,),
        [pl.BlockSpec(side.shape, lambda i: (0, 0))] + piece_specs + scale_specs,
        out_spec,
        jax.ShapeDtypeStruct(shape, F32),
        (side, *[a for parts, _ in pieces for a in parts], row_scale, col_scale),
        after,
        carry,
        name="write_update",
    )


def gcd(a, b):
    while b:
        a, b = b, a % b
    return a


def power_of_two(size):
    return size & (size - 1) == 0


def all_sum(value, axis, during=()):
    size = lax.axis_size(axis)
    if not power_of_two(size):
        return lax.psum(value, axis)
    bit, turn = 1, 0
    while bit < size:
        arrived = lax.ppermute(value, axis, [(i, i ^ bit) for i in range(size)])
        if turn < len(during):
            value = during[turn](value)
        value = value + arrived
        bit, turn = bit * 2, turn + 1
    return value


def gather_rows(share, axis):
    size = lax.axis_size(axis)
    if not power_of_two(size):
        return lax.all_gather(share, axis, axis=0, tiled=True)
    blocks = [share]
    for bits in range(1, size):
        blocks.append(lax.ppermute(share, axis, [(i, i ^ bits) for i in range(size)]))
    return jnp.concatenate(blocks)


def scatter_rows(partial, axis):
    size = lax.axis_size(axis)
    if not power_of_two(size):
        return lax.psum_scatter(partial, axis, scatter_dimension=0, tiled=True).astype(F32)
    share = partial.shape[0] // size
    total = partial[:share].astype(F32)
    for bits in range(1, size):
        part = partial[bits * share : (bits + 1) * share]
        total = total + lax.ppermute(part, axis, [(i, i ^ bits) for i in range(size)]).astype(F32)
    return total


def body(patches, ln_gain, weight_in, weight_out, upstream, row_in, col_in, row_out, col_out):
    gx, gy = lax.axis_size("gx"), lax.axis_size("gy")
    width = weight_in.shape[1]
    features = patches.shape[1]
    model, hidden_units = features * gx, width * gy
    widths = [width * n // 12 for n in RUNS]
    starts = [sum(widths[:n]) for n in range(len(widths))]

    state = [lax.axis_index("gx").astype(jnp.int32)[None]]

    def run(function, *args, **kwargs):
        results, carried = function(*args, carry=[state[0]], **kwargs)
        state[0] = carried[0]
        return results

    def share_sum(partial):
        return lax.psum_scatter(partial, "gx", scatter_dimension=0, tiled=True)

    up_full = gather_rows(upstream, "gy")
    x_float = patches.astype(F32)
    stats = all_sum(jnp.stack([jnp.sum(x_float, axis=1), jnp.sum(x_float * x_float, axis=1)]), "gx") / model
    row_mean = stats[0][:, None]
    inv_std = lax.rsqrt(stats[1][:, None] - row_mean * row_mean + 1e-06)
    unit = (x_float - row_mean) * inv_std
    normed = (unit * ln_gain[None, :]).astype(BF16)
    normed_full = gather_rows(normed, "gy")

    grad = share_sum(run(project, up_full, weight_out, 0, width, 1))
    pre = share_sum(run(project, normed_full, weight_in, 0, width, 0))
    up_side, normed_side = up_full.T, normed_full.T

    def all_rows(share):
        return [lax.all_gather(share, "gx", axis=0)]

    outer = {"pieces": [], "cols": [], "sums": None}
    inner = {"pieces": [], "cols": [], "sums": None}

    def take(side, parts, left, weight, start, dim):
        cols, lanes, product = run(consume, parts, 0, left, weight, start, dim, side["sums"])
        side["pieces"].append((parts, 0))
        side["cols"].append(cols[0])
        side["sums"] = (lanes, product)

    hidden, slope = run(activate, pre)
    hidden_parts = all_rows(hidden)
    act = (grad.astype(F32) * slope).astype(BF16)[None]
    act_parts = [all_rows(act[:, :, s : s + w]) for s, w in zip(starts, widths)]
    take(outer, hidden_parts, up_side, weight_out, 0, 0)

    def factors(feature_sum, hidden_sum, grand, along_features, along_hidden):
        feature_new = 0.9 * along_features + 0.1 * (feature_sum / hidden_units + 1e-30)
        hidden_new = 0.9 * along_hidden + 0.1 * (hidden_sum / model + 1e-30)
        return feature_new, hidden_new, 0.1 * (grand / model / hidden_units + 1e-30)

    def lane_sums(lanes, extra):
        feature_sum = jnp.sum(lanes, axis=1)
        return jnp.concatenate([feature_sum, jnp.full((64,), jnp.sum(feature_sum)), jnp.full((64,), extra)])

    lanes, branch = outer["sums"]
    feature_sum = all_sum(lane_sums(lanes, jnp.sum(row_out)), "gy")
    hidden_sum = all_sum(jnp.concatenate(outer["cols"] + [feature_sum[features:]]), "gx")
    col_out_new, row_out_new, mean_out = factors(feature_sum[:features], hidden_sum[:width], hidden_sum[width], col_out, row_out)
    mean_out = 0.9 * (feature_sum[features + 64] / hidden_units) + mean_out
    row_scale, col_scale = (lax.rsqrt(row_out_new) * jnp.sqrt(mean_out))[None, :], lax.rsqrt(col_out_new)[None, :]
    output = (x_float + scatter_rows(branch.astype(BF16), "gy")).astype(BF16)

    update_out = run(write_update, up_full, outer["pieces"], row_scale, col_scale, True, after=[output])

    for parts, start in zip(act_parts, starts):
        take(inner, parts, normed_side, weight_in, start, 1)
    lanes, normed_grad = inner["sums"]
    feature_sum = all_sum(lane_sums(lanes, 0.0), "gy")
    scaled = scatter_rows(normed_grad.astype(BF16), "gy") * ln_gain[None, :]
    norm_sums = [jnp.sum(scaled, axis=1), jnp.sum(scaled * unit, axis=1)]
    hidden_sum = jnp.concatenate(inner["cols"] + [feature_sum[features:], jnp.full((128,), jnp.sum(row_in))] + norm_sums)
    hidden_sum = all_sum(hidden_sum, "gx")
    row_in_new, col_in_new, mean_in = factors(feature_sum[:features], hidden_sum[:width], hidden_sum[width], row_in, col_in)
    mean_in = 0.9 * (hidden_sum[width + 128] / model) + mean_in
    row_scale, col_scale = lax.rsqrt(row_in_new)[:, None], (lax.rsqrt(col_in_new) * jnp.sqrt(mean_in))[None, :]
    update_in = run(write_update, normed_side, inner["pieces"], row_scale, col_scale, False)
    means = hidden_sum[width + 256 :].reshape(2, -1, 1) / model
    input_grad = upstream.astype(F32) + inv_std * (scaled - means[0] - unit * means[1])
    return (output, input_grad, update_in, update_out)


def solution(mesh):
    in_specs = (
        P("gy", "gx"),
        P("gx"),
        P("gx", "gy"),
        P("gy", "gx"),
        P("gy", "gx"),
        P("gx"),
        P("gy"),
        P("gy"),
        P("gx"),
    )
    out_specs = (P("gy", "gx"), P("gy", "gx"), P("gx", "gy"), P("gy", "gx"))
    return jax.shard_map(body, mesh=mesh, in_specs=in_specs, out_specs=out_specs, check_vma=False)
```

```python
import functools

import jax
import jax.numpy as jnp
from jax import lax
from jax.experimental import pallas as pl
from jax.experimental.pallas import tpu as pltpu
from jax.sharding import PartitionSpec as P

F32 = jnp.float32
BF16 = jnp.bfloat16
VMEM = 58 * 2**20


def block(total, limit):
    best = 128
    for width in range(128, min(total, limit) + 1, 128):
        if total % width == 0:
            best = width
    return best


def launch(kernel, grid, in_specs, out_specs, out_shape, args, after=(), carry=(), scratch=(), flops=0, name="kernel"):
    many = isinstance(out_shape, list)
    shapes = out_shape if many else [out_shape]
    specs = out_specs if many else [out_specs]
    hidden = len(after) + len(carry)
    idle = [pl.BlockSpec(memory_space=pl.ANY)]

    def wrapped(*refs):
        inputs, rest = refs[: len(args)], refs[len(args) + hidden :]
        kernel(*inputs, *rest[: len(shapes)], *rest[len(shapes) + len(carry) :])

    results = pl.pallas_call(
        wrapped,
        grid=grid,
        in_specs=list(in_specs) + idle * hidden,
        out_specs=specs + idle * len(carry),
        out_shape=shapes + [jax.ShapeDtypeStruct(c.shape, c.dtype) for c in carry],
        input_output_aliases={len(args) + len(after) + n: len(shapes) + n for n in range(len(carry))},
        scratch_shapes=list(scratch),
        compiler_params=pltpu.CompilerParams(vmem_limit_bytes=VMEM),
        cost_estimate=pl.CostEstimate(flops=int(flops), bytes_accessed=int(flops / 300), transcendentals=0),
        name=name,
    )(*args, *after, *carry)
    own = results[: len(shapes)]
    return (list(own) if many else own[0]), list(results[len(shapes) :])


def aligned(width, start, limit):
    step = block(width, limit)
    while start % step:
        step = block(width, step - 128)
    return step, start // step


def project(rows, weight, start, width, dim, after=(), carry=(), limit=1536):
    count, depth = rows.shape
    step, first = aligned(width, start, limit)

    def kernel(x, w, o):
        dims = (((1,), (dim,)), ((), ()))
        o[...] = lax.dot_general(x[...], w[...], dims, preferred_element_type=F32).astype(o.dtype)

    if dim == 0:
        spec = pl.BlockSpec((depth, step), lambda i: (0, first + i))
    else:
        spec = pl.BlockSpec((step, depth), lambda i: (first + i, 0))
    return launch(
        kernel,
        (width // step,),
        [pl.BlockSpec((count, depth), lambda i: (0, 0)), spec],
        pl.BlockSpec((count, step), lambda i: (0, i)),
        jax.ShapeDtypeStruct((count, width), BF16),
        (rows, weight),
        after,
        carry,
        flops=4 * count * depth * width,
        name="project",
    )


def parts_specs(parts, which, step, index):
    blocks, _, rows, _ = parts[0].shape
    return [pl.BlockSpec((blocks, 1, rows, step), lambda i: (0, which, 0, index(i)))] * len(parts)


def whole_rows(refs):
    blocks, _, rows, step = refs[0].shape
    whole = [r[:, 0].reshape(blocks * rows, step) for r in refs]
    return whole[0] if len(whole) == 1 else jnp.concatenate(whole)


def consume(parts, left, weight, dim, after=(), carry=(), limit=2048):
    depth, count = left.shape
    width = parts[0].shape[3]
    step = block(width, limit)

    def kernel(x, w, *rest):
        cols, feature, product, lanes, total = rest[-5:]
        a = whole_rows(rest[:-5])
        g = jnp.dot(x[...], a, preferred_element_type=F32)
        s = g * g
        cols[...] = jnp.sum(s, axis=0, keepdims=True)
        folded = s[:, :128]
        for j in range(1, step // 128):
            folded += s[:, j * 128 : (j + 1) * 128]
        part = lax.dot_general(a, w[...], (((1,), (dim,)), ((), ())), preferred_element_type=F32)

        @pl.when(pl.program_id(0) == 0)
        def _():
            lanes[...] = folded
            total[...] = part

        @pl.when(pl.program_id(0) != 0)
        def _():
            lanes[...] += folded
            total[...] += part

        @pl.when(pl.program_id(0) == width // step - 1)
        def _():
            row = jnp.sum(jnp.transpose(lanes[...]), axis=0, keepdims=True)
            feature[:, :depth] = jnp.broadcast_to(row, (8, depth))
            feature[:, depth:] = jnp.broadcast_to(jnp.sum(row, axis=1, keepdims=True), (8, 128))
            product[...] = total[...].astype(BF16)

    spec = pl.BlockSpec((step, depth), lambda i: (i, 0)) if dim == 0 else pl.BlockSpec((depth, step), lambda i: (0, i))
    return launch(
        kernel,
        (width // step,),
        [pl.BlockSpec((depth, count), lambda i: (0, 0)), spec] + parts_specs(parts, 0, step, lambda i: i),
        [
            pl.BlockSpec((1, step), lambda i: (0, i)),
            pl.BlockSpec((8, depth + 128), lambda i: (0, 0)),
            pl.BlockSpec((count, depth), lambda i: (0, 0)),
        ],
        [
            jax.ShapeDtypeStruct((1, width), F32),
            jax.ShapeDtypeStruct((8, depth + 128), F32),
            jax.ShapeDtypeStruct((count, depth), BF16),
        ],
        (left, weight, *parts),
        after,
        carry,
        scratch=[pltpu.VMEM((depth, 128), F32), pltpu.VMEM((count, depth), F32)],
        flops=8 * count * depth * width,
        name="consume",
    )


def gelu(pre):
    phi = 0.5 * (1.0 + lax.erf(pre * 0.7071067811865476))
    slope = phi + pre * jnp.exp(-0.5 * pre * pre) * 0.3989422804014327
    return pre * phi, slope


def activate(pre, grad, after=(), carry=()):
    rows, width = pre.shape
    step = block(width, 3072)

    def kernel(p, g, hidden, act):
        value, slope = gelu(p[...].astype(F32))
        hidden[0] = value.astype(BF16)
        act[0] = (g[...].astype(F32) * slope).astype(BF16)

    spec = pl.BlockSpec((rows, step), lambda i: (0, i))
    return launch(
        kernel,
        (width // step,),
        [spec, spec],
        [pl.BlockSpec((1, rows, step), lambda i: (0, 0, i))] * 2,
        [jax.ShapeDtypeStruct((1, rows, width), BF16)] * 2,
        (pre, grad),
        after,
        carry,
        flops=1e9,
        name="activate",
    )


def write_update(side, parts, feature_sum, hidden_sums, before, sizes, hidden_rows, after=(), carry=(), limit=1536):
    total = parts[0].shape[3]
    step = block(total, limit)
    features = side.shape[1] if hidden_rows else side.shape[0]
    model, hidden_units = sizes

    def tall(row):
        return jnp.transpose(jnp.broadcast_to(row, (8, row.shape[1])))[:, :1]

    def kernel(x, *rest):
        across, near_sum, far_sum, near_all, far_all, feature_before, hidden_before, mean_before, o = rest[-9:]
        a = whole_rows(rest[:-9])
        if hidden_rows:
            g = lax.dot_general(a, x[...], (((0,), (0,)), ((), ())), preferred_element_type=F32)
        else:
            g = jnp.dot(x[...], a, preferred_element_type=F32)
        grand = (near_all[:, :1] + far_all[:, :1]) / model / hidden_units + 1e-30
        mean = 0.9 * mean_before[:, :1] + 0.1 * grand
        by_feature = 0.9 * feature_before[...] + 0.1 * (across[:1, :features] / hidden_units + 1e-30)
        by_hidden = 0.9 * hidden_before[...] + 0.1 * ((near_sum[...] + far_sum[...]) / model + 1e-30)
        by_feature = lax.rsqrt(by_feature) * jnp.sqrt(mean)
        by_hidden = lax.rsqrt(by_hidden)
        if hidden_rows:
            o[...] = g * tall(by_hidden) * by_feature
        else:
            o[...] = g * tall(by_feature) * by_hidden

    along_hidden = pl.BlockSpec((1, step), lambda i: (0, i))
    behind = pl.BlockSpec((1, 128), lambda i: (0, total // 128))
    scale_specs = [
        pl.BlockSpec((8, features + 128), lambda i: (0, 0)),
        along_hidden,
        along_hidden,
        behind,
        behind,
        pl.BlockSpec((1, features), lambda i: (0, 0)),
        along_hidden,
        pl.BlockSpec((1, 128), lambda i: (0, 0)),
    ]
    if hidden_rows:
        out_spec = pl.BlockSpec((step, features), lambda i: (i, 0))
        shape = (total, features)
    else:
        out_spec = pl.BlockSpec((features, step), lambda i: (0, i))
        shape = (features, total)
    return launch(
        kernel,
        (total // step,),
        [pl.BlockSpec(side.shape, lambda i: (0, 0))] + parts_specs(parts, 0, step, lambda i: i) + scale_specs,
        out_spec,
        jax.ShapeDtypeStruct(shape, F32),
        (side, *parts, feature_sum, *hidden_sums, *hidden_sums, *before),
        after,
        carry,
        flops=3000 * features * total,
        name="write_update",
    )


def power_of_two(size):
    return size & (size - 1) == 0


def all_sum(value, axis, split=False):
    size = lax.axis_size(axis)
    if not power_of_two(size):
        value = lax.psum(value, axis)
        return (value, jnp.zeros_like(value)) if split else value
    bit = 1
    while bit < size:
        count = min(4, size // bit)
        arrived = [lax.ppermute(value, axis, [(i, i ^ (bit * n)) for i in range(size)]) for n in range(1, count)]
        bit *= count
        if split and bit >= size:
            return functools.reduce(jnp.add, arrived[1:], value), arrived[0]
        value = functools.reduce(jnp.add, arrived, value)
    return (value, jnp.zeros_like(value)) if split else value


def gather_rows(share, axis):
    size = lax.axis_size(axis)
    if not power_of_two(size):
        return lax.all_gather(share, axis, axis=0, tiled=True)
    blocks = [share]
    for bits in range(1, size):
        blocks.append(lax.ppermute(share, axis, [(i, i ^ bits) for i in range(size)]))
    return jnp.concatenate(blocks)


def scatter_rows(partial, axis):
    size = lax.axis_size(axis)
    if not power_of_two(size):
        return lax.psum_scatter(partial, axis, scatter_dimension=0, tiled=True).astype(F32)
    share = partial.shape[0] // size
    total = partial[:share].astype(F32)
    for bits in range(1, size):
        part = partial[bits * share : (bits + 1) * share]
        total = total + lax.ppermute(part, axis, [(i, i ^ bits) for i in range(size)]).astype(F32)
    return total


def body(patches, ln_gain, weight_in, weight_out, upstream, row_in, col_in, row_out, col_out):
    gx, gy = lax.axis_size("gx"), lax.axis_size("gy")
    width = weight_in.shape[1]
    features = patches.shape[1]
    model, hidden_units = features * gx, width * gy

    state = [lax.axis_index("gx").astype(jnp.int32)[None]]

    def run(function, *args, **kwargs):
        results, carried = function(*args, carry=[state[0]], **kwargs)
        state[0] = carried[0]
        return results

    def share_sum(partial):
        return lax.psum_scatter(partial, "gx", scatter_dimension=0, tiled=True)

    up_full = gather_rows(upstream, "gy")
    x_float = patches.astype(F32)
    stats = all_sum(jnp.stack([jnp.sum(x_float, axis=1), jnp.sum(x_float * x_float, axis=1)]), "gx") / model
    row_mean = stats[0][:, None]
    inv_std = lax.rsqrt(stats[1][:, None] - row_mean * row_mean + 1e-06)
    unit = (x_float - row_mean) * inv_std
    normed = (unit * ln_gain[None, :]).astype(BF16)
    normed_full = gather_rows(normed, "gy")

    grad = share_sum(run(project, up_full, weight_out, 0, width, 1))
    pre = share_sum(run(project, normed_full, weight_in, 0, width, 0))
    up_side, normed_side = up_full.T, normed_full.T

    def all_rows(share):
        return [lax.all_gather(share, "gx", axis=0)]

    outer = {"pieces": [], "cols": [], "sums": None}
    inner = {"pieces": [], "cols": [], "sums": None}

    def take(side, parts, left, weight, start, dim):
        cols, lanes, product = run(consume, parts, 0, left, weight, start, dim, side["sums"])
        side["pieces"].append((parts, 0))
        side["cols"].append(cols[0])
        side["sums"] = (lanes, product)

    hidden, act = run(activate, pre, grad)
    act_parts, hidden_parts = all_rows(act), all_rows(hidden)

    def mean_of(factor, axis):
        return jnp.full((1, 128), all_sum(jnp.full((128,), jnp.sum(factor)), axis)[0] / (factor.shape[0] * lax.axis_size(axis)))

    mean_in, mean_out = mean_of(row_in, "gx"), mean_of(row_out, "gy")
    sizes = (float(model), float(hidden_units))

    hidden_sum, feature_sum, normed_grad = run(consume, act_parts, normed_side, weight_in, 1, after=[mean_in, mean_out])
    feature_sum = all_sum(feature_sum, "gy")
    scaled = scatter_rows(normed_grad, "gy") * ln_gain[None, :]
    norm_sums = jnp.concatenate([jnp.sum(scaled, axis=1), jnp.sum(scaled * unit, axis=1)])[None, :]
    hidden_sum = jnp.concatenate([hidden_sum, feature_sum[:1, features:], norm_sums], axis=1)
    hidden_sums = all_sum(hidden_sum, "gx", True)
    means = (hidden_sums[0] + hidden_sums[1])[0, width + 128 :].reshape(2, -1, 1) / model
    input_grad = upstream.astype(F32) + inv_std * (scaled - means[0] - unit * means[1])
    before = (row_in[None, :], col_in[None, :], mean_in)
    update_in = run(
        write_update, normed_side, act_parts, feature_sum, hidden_sums, before, sizes, False, after=[input_grad]
    )

    hidden_sum, feature_sum, branch = run(consume, hidden_parts, up_side, weight_out, 0)
    feature_sum = all_sum(feature_sum, "gy")
    hidden_sums = all_sum(jnp.concatenate([hidden_sum, feature_sum[:1, features:]], axis=1), "gx", True)
    before = (col_out[None, :], row_out[None, :], mean_out)
    update_out = run(write_update, up_full, hidden_parts, feature_sum, hidden_sums, before, sizes, True)
    output = (x_float + scatter_rows(branch, "gy")).astype(BF16)
    return (output, input_grad, update_in, update_out)


def solution(mesh):
    in_specs = (
        P("gy", "gx"),
        P("gx"),
        P("gx", "gy"),
        P("gy", "gx"),
        P("gy", "gx"),
        P("gx"),
        P("gy"),
        P("gy"),
        P("gx"),
    )
    out_specs = (P("gy", "gx"), P("gy", "gx"), P("gx", "gy"), P("gy", "gx"))
    return jax.shard_map(body, mesh=mesh, in_specs=in_specs, out_specs=out_specs, check_vma=False)
```

```python
import functools

import jax
import jax.numpy as jnp
from jax import lax
from jax.experimental import pallas as pl
from jax.experimental.pallas import tpu as pltpu
from jax.sharding import PartitionSpec as P

F32 = jnp.float32
BF16 = jnp.bfloat16
VMEM = 44 * 2**20


def block(total, limit):
    best = 128
    for width in range(128, min(total, limit) + 1, 128):
        if total % width == 0:
            best = width
    return best


def launch(kernel, grid, in_specs, out_specs, out_shape, args, after=(), carry=(), scratch=(), flops=0, name="kernel"):
    many = isinstance(out_shape, list)
    shapes = out_shape if many else [out_shape]
    specs = out_specs if many else [out_specs]
    hidden = len(after) + len(carry)
    idle = [pl.BlockSpec(memory_space=pl.ANY)]

    def wrapped(*refs):
        inputs, rest = refs[: len(args)], refs[len(args) + hidden :]
        kernel(*inputs, *rest[: len(shapes)], *rest[len(shapes) + len(carry) :])

    results = pl.pallas_call(
        wrapped,
        grid=grid,
        in_specs=list(in_specs) + idle * hidden,
        out_specs=specs + idle * len(carry),
        out_shape=shapes + [jax.ShapeDtypeStruct(c.shape, c.dtype) for c in carry],
        input_output_aliases={len(args) + len(after) + n: len(shapes) + n for n in range(len(carry))},
        scratch_shapes=list(scratch),
        compiler_params=pltpu.CompilerParams(vmem_limit_bytes=VMEM),
        cost_estimate=pl.CostEstimate(flops=int(flops), bytes_accessed=int(flops / 300), transcendentals=0),
        name=name,
    )(*args, *after, *carry)
    own = results[: len(shapes)]
    return (list(own) if many else own[0]), list(results[len(shapes) :])


def project(rows, weight, dim, halves=1, after=(), carry=(), limit=1536):
    count, depth = rows.shape
    width = weight.shape[1 - dim]
    step = block(width, limit)
    part_rows = count // halves

    def kernel(x, w, *outs):
        dims = (((1,), (dim,)), ((), ()))
        part = lax.dot_general(x[...], w[...], dims, preferred_element_type=F32).astype(BF16)
        for n, o in enumerate(outs):
            o[...] = part[n * part_rows : (n + 1) * part_rows]

    spec = pl.BlockSpec((depth, step), lambda i: (0, i)) if dim == 0 else pl.BlockSpec((step, depth), lambda i: (i, 0))
    return launch(
        kernel,
        (width // step,),
        [pl.BlockSpec((count, depth), lambda i: (0, 0)), spec],
        [pl.BlockSpec((part_rows, step), lambda i: (0, i))] * halves,
        [jax.ShapeDtypeStruct((part_rows, width), BF16)] * halves,
        (rows, weight),
        after,
        carry,
        flops=4 * count * depth * width,
        name="project",
    )


def parts_specs(parts, which, step, index):
    blocks, _, rows, _ = parts[0].shape
    return [pl.BlockSpec((blocks, 1, rows, step), lambda i: (0, which, 0, index(i)))] * len(parts)


def whole_rows(refs):
    blocks, _, rows, step = refs[0].shape
    whole = [r[:, 0].reshape(blocks * rows, step) for r in refs]
    return whole[0] if len(whole) == 1 else jnp.concatenate(whole)


def consume(parts, side, weight, dim, hidden_rows, after=(), carry=(), limit=1536):
    count, depth = side.shape if hidden_rows else side.shape[::-1]
    width = parts[0].shape[3]
    step = block(width, limit)

    def fold(squares):
        folded = squares[:, :128]
        for j in range(1, squares.shape[1] // 128):
            folded += squares[:, j * 128 : (j + 1) * 128]
        return folded

    def kernel(x, w, *rest):
        grad, cols, feature, product, sums, total = rest[-6:]
        i = pl.program_id(0)
        a = whole_rows(rest[:-6])
        here = pl.ds(pl.multiple_of(i * step, step), step)
        if hidden_rows:
            g = lax.dot_general(a, x[...], (((0,), (0,)), ((), ())), preferred_element_type=F32)
            grad[here, :] = g.astype(BF16)
            s = g * g
            cols[...] = jnp.sum(jnp.transpose(fold(s)), axis=0, keepdims=True)
            across = jnp.broadcast_to(jnp.sum(s, axis=0, keepdims=True), (8, depth))
        else:
            g = jnp.dot(x[...], a, preferred_element_type=F32)
            grad[:, here] = g.astype(BF16)
            s = g * g
            cols[...] = jnp.sum(s, axis=0, keepdims=True)
            across = fold(s)
        part = lax.dot_general(a, w[...], (((1,), (dim,)), ((), ())), preferred_element_type=F32)

        @pl.when(i == 0)
        def _():
            sums[...] = across
            total[...] = part

        @pl.when(i != 0)
        def _():
            sums[...] += across
            total[...] += part

        @pl.when(i == width // step - 1)
        def _():
            row = sums[:1, :] if hidden_rows else jnp.sum(jnp.transpose(sums[...]), axis=0, keepdims=True)
            feature[:, :depth] = jnp.broadcast_to(row, (8, depth))
            feature[:, depth:] = jnp.broadcast_to(jnp.sum(row, axis=1, keepdims=True), (8, 128))
            product[...] = total[...].astype(BF16)

    spec = pl.BlockSpec((step, depth), lambda i: (i, 0)) if dim == 0 else pl.BlockSpec((depth, step), lambda i: (0, i))
    return launch(
        kernel,
        (width // step,),
        [pl.BlockSpec(side.shape, lambda i: (0, 0)), spec] + parts_specs(parts, 0, step, lambda i: i),
        [
            pl.BlockSpec(memory_space=pltpu.VMEM),
            pl.BlockSpec((1, step), lambda i: (0, i)),
            pl.BlockSpec((8, depth + 128), lambda i: (0, 0)),
            pl.BlockSpec((count, depth), lambda i: (0, 0)),
        ],
        [
            pltpu.VMEM((width, depth) if hidden_rows else (depth, width), BF16),
            jax.ShapeDtypeStruct((1, width), F32),
            jax.ShapeDtypeStruct((8, depth + 128), F32),
            jax.ShapeDtypeStruct((count, depth), BF16),
        ],
        (side, weight, *parts),
        after,
        carry,
        scratch=[pltpu.VMEM((8, depth) if hidden_rows else (depth, 128), F32), pltpu.VMEM((count, depth), F32)],
        flops=8 * count * depth * width,
        name="consume",
    )


def gelu(pre):
    phi = 0.5 * (1.0 + lax.erf(pre * 0.7071067811865476))
    slope = phi + pre * jnp.exp(-0.5 * pre * pre) * 0.3989422804014327
    return pre * phi, slope


def activate(pre, grad, after=(), carry=()):
    rows, width = pre.shape
    step = block(width, 3072)

    def kernel(p, g, hidden, act):
        value, slope = gelu(p[...].astype(F32))
        hidden[0] = value.astype(BF16)
        act[0] = (g[...].astype(F32) * slope).astype(BF16)

    spec = pl.BlockSpec((rows, step), lambda i: (0, i))
    return launch(
        kernel,
        (width // step,),
        [spec, spec],
        [pl.BlockSpec((1, rows, step), lambda i: (0, 0, i))] * 2,
        [jax.ShapeDtypeStruct((1, rows, width), BF16)] * 2,
        (pre, grad),
        after,
        carry,
        flops=1e9,
        name="activate",
    )


def settle(after, carry):
    return launch(lambda: None, (1,), [], [], [], (), after, carry, name="settle")


def write_update(grad, feature_sum, hidden_sums, before, sizes, hidden_rows, after=(), carry=(), limit=768):
    total, features = grad.shape if hidden_rows else grad.shape[::-1]
    step = block(total, limit)
    model, hidden_units = sizes

    def tall(row):
        return jnp.transpose(jnp.broadcast_to(row, (8, row.shape[1])))[:, :1]

    def kernel(whole, across, near_sum, far_sum, near_all, far_all, feature_before, hidden_before, mean_before, o):
        here = pl.ds(pl.multiple_of(pl.program_id(0) * step, step), step)
        g = (whole[here, :] if hidden_rows else whole[:, here]).astype(F32)
        grand = (near_all[:, :1] + far_all[:, :1]) / model / hidden_units + 1e-30
        mean = 0.9 * mean_before[:, :1] + 0.1 * grand
        by_feature = 0.9 * feature_before[...] + 0.1 * (across[:1, :features] / hidden_units + 1e-30)
        by_hidden = 0.9 * hidden_before[...] + 0.1 * ((near_sum[...] + far_sum[...]) / model + 1e-30)
        by_feature = lax.rsqrt(by_feature) * jnp.sqrt(mean)
        by_hidden = lax.rsqrt(by_hidden)
        if hidden_rows:
            o[...] = g * tall(by_hidden) * by_feature
        else:
            o[...] = g * tall(by_feature) * by_hidden

    along_hidden = pl.BlockSpec((1, step), lambda i: (0, i))
    behind = pl.BlockSpec((1, 128), lambda i: (0, total // 128))
    scale_specs = [
        pl.BlockSpec((8, features + 128), lambda i: (0, 0)),
        along_hidden,
        along_hidden,
        behind,
        behind,
        pl.BlockSpec((1, features), lambda i: (0, 0)),
        along_hidden,
        pl.BlockSpec((1, 128), lambda i: (0, 0)),
    ]
    if hidden_rows:
        out_spec = pl.BlockSpec((step, features), lambda i: (i, 0))
        shape = (total, features)
    else:
        out_spec = pl.BlockSpec((features, step), lambda i: (0, i))
        shape = (features, total)
    return launch(
        kernel,
        (total // step,),
        [pl.BlockSpec(memory_space=pltpu.VMEM)] + scale_specs,
        out_spec,
        jax.ShapeDtypeStruct(shape, F32),
        (grad, feature_sum, *hidden_sums, *hidden_sums, *before),
        after,
        carry,
        flops=1500 * features * total,
        name="write_update",
    )


def power_of_two(size):
    return size & (size - 1) == 0


def all_sum(value, axis, split=False):
    size = lax.axis_size(axis)
    if not power_of_two(size):
        value = lax.psum(value, axis)
        return (value, jnp.zeros_like(value)) if split else value
    bit = 1
    while bit < size:
        count = min(4, size // bit)
        arrived = [lax.ppermute(value, axis, [(i, i ^ (bit * n)) for i in range(size)]) for n in range(1, count)]
        bit *= count
        if split and bit >= size:
            return functools.reduce(jnp.add, arrived[1:], value), arrived[0]
        value = functools.reduce(jnp.add, arrived, value)
    return (value, jnp.zeros_like(value)) if split else value


def gather_rows(share, axis):
    size = lax.axis_size(axis)
    if not power_of_two(size):
        return lax.all_gather(share, axis, axis=0, tiled=True)
    blocks = [share]
    for bits in range(1, size):
        blocks.append(lax.ppermute(share, axis, [(i, i ^ bits) for i in range(size)]))
    return jnp.concatenate(blocks)


def scatter_rows(partial, axis):
    size = lax.axis_size(axis)
    if not power_of_two(size):
        return lax.psum_scatter(partial, axis, scatter_dimension=0, tiled=True).astype(F32)
    share = partial.shape[0] // size
    total = partial[:share].astype(F32)
    for bits in range(1, size):
        part = partial[bits * share : (bits + 1) * share]
        total = total + lax.ppermute(part, axis, [(i, i ^ bits) for i in range(size)]).astype(F32)
    return total


def body(patches, ln_gain, weight_in, weight_out, upstream, row_in, col_in, row_out, col_out):
    gx, gy = lax.axis_size("gx"), lax.axis_size("gy")
    width = weight_in.shape[1]
    features = patches.shape[1]
    model, hidden_units = features * gx, width * gy

    core = lax.axis_index("gx") % 2

    state = [lax.axis_index("gx").astype(jnp.int32)[None]]

    def run(function, *args, **kwargs):
        results, carried = function(*args, carry=[state[0]], **kwargs)
        state[0] = carried[0]
        return results

    def share_sum(partial):
        return lax.psum_scatter(partial, "gx", scatter_dimension=0, tiled=True)

    up_full = gather_rows(upstream, "gy")
    x_float = patches.astype(F32)
    stats = all_sum(jnp.stack([jnp.sum(x_float, axis=1), jnp.sum(x_float * x_float, axis=1)]), "gx") / model
    row_mean = stats[0][:, None]
    inv_std = lax.rsqrt(stats[1][:, None] - row_mean * row_mean + 1e-06)
    unit = (x_float - row_mean) * inv_std
    normed = (unit * ln_gain[None, :]).astype(BF16)
    normed_full = gather_rows(normed, "gy")

    (grad,) = run(project, up_full, weight_out, 1)
    grad = share_sum(grad)

    own = lax.dynamic_index_in_dim(normed_full.reshape(gx // 2, 2, -1, features), core, 1, keepdims=False)
    other = lax.dynamic_index_in_dim(normed_full.reshape(gx // 2, 2, -1, features), 1 - core, 1, keepdims=False)
    halves = jnp.concatenate([own, other]).reshape(normed_full.shape)
    pre_own, pre_other = run(project, halves, weight_in, 0, 2)
    pre_other = lax.ppermute(pre_other, "gx", [(i, i ^ 1) for i in range(gx)])
    both = (pre_own.astype(F32) + pre_other.astype(F32)).astype(BF16)
    (both,) = settle([grad], [both])[1]
    pre = lax.psum_scatter(
        both,
        "gx",
        scatter_dimension=0,
        axis_index_groups=[list(range(c, gx, 2)) for c in (0, 1)],
        tiled=True,
    )
    normed_side = normed_full.T

    def all_rows(share):
        return [lax.all_gather(share, "gx", axis=0)]

    hidden, act = run(activate, pre, grad)
    act_parts, hidden_parts = all_rows(act), all_rows(hidden)

    def mean_of(factor, axis):
        return jnp.full((1, 128), all_sum(jnp.full((128,), jnp.sum(factor)), axis)[0] / (factor.shape[0] * lax.axis_size(axis)))

    mean_in, mean_out = mean_of(row_in, "gx"), mean_of(row_out, "gy")
    sizes = (float(model), float(hidden_units))

    grad_in, hidden_sum, feature_sum, normed_grad = run(
        consume, act_parts, normed_side, weight_in, 1, False, after=[mean_in, mean_out]
    )
    feature_sum = all_sum(feature_sum, "gy")
    scaled = scatter_rows(normed_grad, "gy") * ln_gain[None, :]
    norm_sums = jnp.concatenate([jnp.sum(scaled, axis=1), jnp.sum(scaled * unit, axis=1)])[None, :]
    hidden_sum = jnp.concatenate([hidden_sum, feature_sum[:1, features:], norm_sums], axis=1)
    hidden_sums = all_sum(hidden_sum, "gx", True)
    means = (hidden_sums[0] + hidden_sums[1])[0, width + 128 :].reshape(2, -1, 1) / model
    input_grad = upstream.astype(F32) + inv_std * (scaled - means[0] - unit * means[1])
    before = (row_in[None, :], col_in[None, :], mean_in)
    update_in = run(write_update, grad_in, feature_sum, hidden_sums, before, sizes, False, after=[input_grad])

    grad_out, hidden_sum, feature_sum, branch = run(consume, hidden_parts, up_full, weight_out, 0, True)
    feature_sum = all_sum(feature_sum, "gy")
    hidden_sums = all_sum(jnp.concatenate([hidden_sum, feature_sum[:1, features:]], axis=1), "gx", True)
    before = (col_out[None, :], row_out[None, :], mean_out)
    update_out = run(write_update, grad_out, feature_sum, hidden_sums, before, sizes, True)
    output = (x_float + scatter_rows(branch, "gy")).astype(BF16)
    return (output, input_grad, update_in, update_out)


def solution(mesh):
    in_specs = (
        P("gy", "gx"),
        P("gx"),
        P("gx", "gy"),
        P("gy", "gx"),
        P("gy", "gx"),
        P("gx"),
        P("gy"),
        P("gy"),
        P("gx"),
    )
    out_specs = (P("gy", "gx"), P("gy", "gx"), P("gx", "gy"), P("gy", "gx"))
    return jax.shard_map(body, mesh=mesh, in_specs=in_specs, out_specs=out_specs, check_vma=False)
```

```python
import functools

import jax
import jax.numpy as jnp
from jax import lax
from jax.experimental import pallas as pl
from jax.experimental.pallas import tpu as pltpu
from jax.sharding import PartitionSpec as P

F32 = jnp.float32
BF16 = jnp.bfloat16
VMEM = 44 * 2**20


def block(total, limit):
    best = 128
    for width in range(128, min(total, limit) + 1, 128):
        if total % width == 0:
            best = width
    return best


def launch(kernel, grid, in_specs, out_specs, out_shape, args, after=(), carry=(), scratch=(), flops=0, vmem=VMEM, name="kernel"):
    many = isinstance(out_shape, list)
    shapes = out_shape if many else [out_shape]
    specs = out_specs if many else [out_specs]
    hidden = len(after) + len(carry)
    idle = [pl.BlockSpec(memory_space=pl.ANY)]

    def wrapped(*refs):
        inputs, rest = refs[: len(args)], refs[len(args) + hidden :]
        kernel(*inputs, *rest[: len(shapes)], *rest[len(shapes) + len(carry) :])

    results = pl.pallas_call(
        wrapped,
        grid=grid,
        in_specs=list(in_specs) + idle * hidden,
        out_specs=specs + idle * len(carry),
        out_shape=shapes + [jax.ShapeDtypeStruct(c.shape, c.dtype) for c in carry],
        input_output_aliases={len(args) + len(after) + n: len(shapes) + n for n in range(len(carry))},
        scratch_shapes=list(scratch),
        compiler_params=pltpu.CompilerParams(vmem_limit_bytes=vmem),
        cost_estimate=pl.CostEstimate(flops=int(flops), bytes_accessed=int(flops / 300), transcendentals=0),
        name=name,
    )(*args, *after, *carry)
    own = results[: len(shapes)]
    return (list(own) if many else own[0]), list(results[len(shapes) :])


def project(rows, weight, dim, halves=1, after=(), carry=(), limit=1536):
    count, depth = rows.shape
    width = weight.shape[1 - dim]
    step = block(width, limit)
    part_rows = count // halves

    def kernel(x, w, *outs):
        dims = (((1,), (dim,)), ((), ()))
        part = lax.dot_general(x[...], w[...], dims, preferred_element_type=F32).astype(BF16)
        for n, o in enumerate(outs):
            o[...] = part[n * part_rows : (n + 1) * part_rows]

    spec = pl.BlockSpec((depth, step), lambda i: (0, i)) if dim == 0 else pl.BlockSpec((step, depth), lambda i: (i, 0))
    return launch(
        kernel,
        (width // step,),
        [pl.BlockSpec((count, depth), lambda i: (0, 0)), spec],
        [pl.BlockSpec((part_rows, step), lambda i: (0, i))] * halves,
        [jax.ShapeDtypeStruct((part_rows, width), BF16)] * halves,
        (rows, weight),
        after,
        carry,
        flops=4 * count * depth * width,
        vmem=58 * 2**20,
        name="project",
    )


def parts_specs(parts, which, step, index):
    blocks, _, rows, _ = parts[0].shape
    return [pl.BlockSpec((blocks, 1, rows, step), lambda i: (0, which, 0, index(i)))] * len(parts)


def whole_rows(refs):
    blocks, _, rows, step = refs[0].shape
    whole = [r[:, 0].reshape(blocks * rows, step) for r in refs]
    return whole[0] if len(whole) == 1 else jnp.concatenate(whole)


def consume(parts, side, weight, dim, hidden_rows, after=(), carry=(), limit=1536):
    count, depth = side.shape if hidden_rows else side.shape[::-1]
    width = parts[0].shape[3]
    step = block(width, limit)

    def fold(squares):
        folded = squares[:, :128]
        for j in range(1, squares.shape[1] // 128):
            folded += squares[:, j * 128 : (j + 1) * 128]
        return folded

    def kernel(x, w, *rest):
        grad, cols, feature, product, sums, total = rest[-6:]
        i = pl.program_id(0)
        a = whole_rows(rest[:-6])
        here = pl.ds(pl.multiple_of(i * step, step), step)
        if hidden_rows:
            g = lax.dot_general(a, x[...], (((0,), (0,)), ((), ())), preferred_element_type=F32)
            grad[here, :] = g.astype(BF16)
            s = g * g
            cols[...] = jnp.sum(jnp.transpose(fold(s)), axis=0, keepdims=True)
            across = jnp.broadcast_to(jnp.sum(s, axis=0, keepdims=True), (8, depth))
        else:
            g = jnp.dot(x[...], a, preferred_element_type=F32)
            grad[:, here] = g.astype(BF16)
            s = g * g
            cols[...] = jnp.sum(s, axis=0, keepdims=True)
            across = fold(s)
        part = lax.dot_general(a, w[...], (((1,), (dim,)), ((), ())), preferred_element_type=F32)

        @pl.when(i == 0)
        def _():
            sums[...] = across
            total[...] = part

        @pl.when(i != 0)
        def _():
            sums[...] += across
            total[...] += part

        @pl.when(i == width // step - 1)
        def _():
            row = sums[:1, :] if hidden_rows else jnp.sum(jnp.transpose(sums[...]), axis=0, keepdims=True)
            feature[:, :depth] = jnp.broadcast_to(row, (8, depth))
            feature[:, depth:] = jnp.broadcast_to(jnp.sum(row, axis=1, keepdims=True), (8, 128))
            product[...] = total[...].astype(BF16)

    spec = pl.BlockSpec((step, depth), lambda i: (i, 0)) if dim == 0 else pl.BlockSpec((depth, step), lambda i: (0, i))
    return launch(
        kernel,
        (width // step,),
        [pl.BlockSpec(side.shape, lambda i: (0, 0)), spec] + parts_specs(parts, 0, step, lambda i: i),
        [
            pl.BlockSpec(memory_space=pltpu.VMEM),
            pl.BlockSpec((1, step), lambda i: (0, i)),
            pl.BlockSpec((8, depth + 128), lambda i: (0, 0)),
            pl.BlockSpec((count, depth), lambda i: (0, 0)),
        ],
        [
            pltpu.VMEM((width, depth) if hidden_rows else (depth, width), BF16),
            jax.ShapeDtypeStruct((1, width), F32),
            jax.ShapeDtypeStruct((8, depth + 128), F32),
            jax.ShapeDtypeStruct((count, depth), BF16),
        ],
        (side, weight, *parts),
        after,
        carry,
        scratch=[pltpu.VMEM((8, depth) if hidden_rows else (depth, 128), F32), pltpu.VMEM((count, depth), F32)],
        flops=8 * count * depth * width,
        name="consume",
    )


def gelu(pre):
    phi = 0.5 * (1.0 + lax.erf(pre * 0.7071067811865476))
    slope = phi + pre * jnp.exp(-0.5 * pre * pre) * 0.3989422804014327
    return pre * phi, slope


def activate(pre, grad, after=(), carry=()):
    rows, width = pre.shape
    step = block(width, 3072)

    def kernel(p, g, hidden, act):
        value, slope = gelu(p[...].astype(F32))
        hidden[0] = value.astype(BF16)
        act[0] = (g[...].astype(F32) * slope).astype(BF16)

    spec = pl.BlockSpec((rows, step), lambda i: (0, i))
    return launch(
        kernel,
        (width // step,),
        [spec, spec],
        [pl.BlockSpec((1, rows, step), lambda i: (0, 0, i))] * 2,
        [jax.ShapeDtypeStruct((1, rows, width), BF16)] * 2,
        (pre, grad),
        after,
        carry,
        flops=1e9,
        vmem=58 * 2**20,
        name="activate",
    )


def settle(after, carry):
    return launch(lambda: None, (1,), [], [], [], (), after, carry, vmem=60 * 2**20, name="settle")


def write_update(grad, feature_sum, hidden_sums, before, sizes, hidden_rows, after=(), carry=(), limit=1536):
    total, features = grad.shape if hidden_rows else grad.shape[::-1]
    step = block(total, limit)
    model, hidden_units = sizes

    def tall(row):
        return jnp.transpose(jnp.broadcast_to(row, (8, row.shape[1])))[:, :1]

    def kernel(whole, across, near_sum, far_sum, near_all, far_all, feature_before, hidden_before, mean_before, o):
        here = pl.ds(pl.multiple_of(pl.program_id(0) * step, step), step)
        g = (whole[here, :] if hidden_rows else whole[:, here]).astype(F32)
        grand = (near_all[:, :1] + far_all[:, :1]) / model / hidden_units + 1e-30
        mean = 0.9 * mean_before[:, :1] + 0.1 * grand
        by_feature = 0.9 * feature_before[...] + 0.1 * (across[:1, :features] / hidden_units + 1e-30)
        by_hidden = 0.9 * hidden_before[...] + 0.1 * ((near_sum[...] + far_sum[...]) / model + 1e-30)
        by_feature = lax.rsqrt(by_feature) * jnp.sqrt(mean)
        by_hidden = lax.rsqrt(by_hidden)
        if hidden_rows:
            o[...] = g * tall(by_hidden) * by_feature
        else:
            o[...] = g * tall(by_feature) * by_hidden

    along_hidden = pl.BlockSpec((1, step), lambda i: (0, i))
    behind = pl.BlockSpec((1, 128), lambda i: (0, total // 128))
    scale_specs = [
        pl.BlockSpec((8, features + 128), lambda i: (0, 0)),
        along_hidden,
        along_hidden,
        behind,
        behind,
        pl.BlockSpec((1, features), lambda i: (0, 0)),
        along_hidden,
        pl.BlockSpec((1, 128), lambda i: (0, 0)),
    ]
    if hidden_rows:
        out_spec = pl.BlockSpec((step, features), lambda i: (i, 0))
        shape = (total, features)
    else:
        out_spec = pl.BlockSpec((features, step), lambda i: (0, i))
        shape = (features, total)
    return launch(
        kernel,
        (total // step,),
        [pl.BlockSpec(memory_space=pltpu.VMEM)] + scale_specs,
        out_spec,
        jax.ShapeDtypeStruct(shape, F32),
        (grad, feature_sum, *hidden_sums, *hidden_sums, *before),
        after,
        carry,
        flops=1500 * features * total,
        name="write_update",
    )


def power_of_two(size):
    return size & (size - 1) == 0


def all_sum(value, axis, split=False):
    size = lax.axis_size(axis)
    if not power_of_two(size):
        value = lax.psum(value, axis)
        return (value, jnp.zeros_like(value)) if split else value
    bit = 1
    while bit < size:
        count = min(4, size // bit)
        arrived = [lax.ppermute(value, axis, [(i, i ^ (bit * n)) for i in range(size)]) for n in range(1, count)]
        bit *= count
        if split and bit >= size:
            return functools.reduce(jnp.add, arrived[1:], value), arrived[0]
        value = functools.reduce(jnp.add, arrived, value)
    return (value, jnp.zeros_like(value)) if split else value


def gather_rows(share, axis):
    size = lax.axis_size(axis)
    if not power_of_two(size):
        return lax.all_gather(share, axis, axis=0, tiled=True)
    blocks = [share]
    for bits in range(1, size):
        blocks.append(lax.ppermute(share, axis, [(i, i ^ bits) for i in range(size)]))
    return jnp.concatenate(blocks)


def scatter_rows(partial, axis):
    size = lax.axis_size(axis)
    if not power_of_two(size):
        return lax.psum_scatter(partial, axis, scatter_dimension=0, tiled=True).astype(F32)
    share = partial.shape[0] // size
    total = partial[:share].astype(F32)
    for bits in range(1, size):
        part = partial[bits * share : (bits + 1) * share]
        total = total + lax.ppermute(part, axis, [(i, i ^ bits) for i in range(size)]).astype(F32)
    return total


def body(patches, ln_gain, weight_in, weight_out, upstream, row_in, col_in, row_out, col_out):
    gx, gy = lax.axis_size("gx"), lax.axis_size("gy")
    width = weight_in.shape[1]
    features = patches.shape[1]
    model, hidden_units = features * gx, width * gy

    core = lax.axis_index("gx") % 2

    state = [lax.axis_index("gx").astype(jnp.int32)[None]]

    def run(function, *args, **kwargs):
        results, carried = function(*args, carry=[state[0]], **kwargs)
        state[0] = carried[0]
        return results

    def share_sum(partial):
        return lax.psum_scatter(partial, "gx", scatter_dimension=0, tiled=True)

    up_full = gather_rows(upstream, "gy")
    x_float = patches.astype(F32)
    stats = all_sum(jnp.stack([jnp.sum(x_float, axis=1), jnp.sum(x_float * x_float, axis=1)]), "gx") / model
    row_mean = stats[0][:, None]
    inv_std = lax.rsqrt(stats[1][:, None] - row_mean * row_mean + 1e-06)
    unit = (x_float - row_mean) * inv_std
    normed = (unit * ln_gain[None, :]).astype(BF16)
    normed_full = gather_rows(normed, "gy")

    (grad,) = run(project, up_full, weight_out, 1)
    grad = share_sum(grad)

    own = lax.dynamic_index_in_dim(normed_full.reshape(gx // 2, 2, -1, features), core, 1, keepdims=False)
    other = lax.dynamic_index_in_dim(normed_full.reshape(gx // 2, 2, -1, features), 1 - core, 1, keepdims=False)
    halves = jnp.concatenate([own, other]).reshape(normed_full.shape)
    pre_own, pre_other = run(project, halves, weight_in, 0, 2)
    pre_other = lax.ppermute(pre_other, "gx", [(i, i ^ 1) for i in range(gx)])
    both = (pre_own.astype(F32) + pre_other.astype(F32)).astype(BF16)
    (both,) = settle([grad], [both])[1]
    pre = lax.psum_scatter(
        both,
        "gx",
        scatter_dimension=0,
        axis_index_groups=[list(range(c, gx, 2)) for c in (0, 1)],
        tiled=True,
    )
    normed_side = normed_full.T

    def all_rows(share):
        return [lax.all_gather(share, "gx", axis=0)]

    hidden, act = run(activate, pre, grad)
    act_parts, hidden_parts = all_rows(act), all_rows(hidden)

    def mean_of(factor, axis):
        return jnp.full((1, 128), all_sum(jnp.full((128,), jnp.sum(factor)), axis)[0] / (factor.shape[0] * lax.axis_size(axis)))

    mean_in, mean_out = mean_of(row_in, "gx"), mean_of(row_out, "gy")
    sizes = (float(model), float(hidden_units))

    grad_in, hidden_sum, feature_sum, normed_grad = run(
        consume, act_parts, normed_side, weight_in, 1, False, after=[mean_in, mean_out]
    )
    feature_sum = all_sum(feature_sum, "gy")
    scaled = scatter_rows(normed_grad, "gy") * ln_gain[None, :]
    norm_sums = jnp.concatenate([jnp.sum(scaled, axis=1), jnp.sum(scaled * unit, axis=1)])[None, :]
    hidden_sum = jnp.concatenate([hidden_sum, feature_sum[:1, features:], norm_sums], axis=1)
    hidden_sums = all_sum(hidden_sum, "gx", True)
    means = (hidden_sums[0] + hidden_sums[1])[0, width + 128 :].reshape(2, -1, 1) / model
    input_grad = upstream.astype(F32) + inv_std * (scaled - means[0] - unit * means[1])
    before = (row_in[None, :], col_in[None, :], mean_in)
    update_in = run(write_update, grad_in, feature_sum, hidden_sums, before, sizes, False, after=[input_grad])

    grad_out, hidden_sum, feature_sum, branch = run(consume, hidden_parts, up_full, weight_out, 0, True)
    feature_sum = all_sum(feature_sum, "gy")
    hidden_sums = all_sum(jnp.concatenate([hidden_sum, feature_sum[:1, features:]], axis=1), "gx", True)
    before = (col_out[None, :], row_out[None, :], mean_out)
    update_out = run(write_update, grad_out, feature_sum, hidden_sums, before, sizes, True)
    output = (x_float + scatter_rows(branch, "gy")).astype(BF16)
    return (output, input_grad, update_in, update_out)


def solution(mesh):
    in_specs = (
        P("gy", "gx"),
        P("gx"),
        P("gx", "gy"),
        P("gy", "gx"),
        P("gy", "gx"),
        P("gx"),
        P("gy"),
        P("gy"),
        P("gx"),
    )
    out_specs = (P("gy", "gx"), P("gy", "gx"), P("gx", "gy"), P("gy", "gx"))
    return jax.shard_map(body, mesh=mesh, in_specs=in_specs, out_specs=out_specs, check_vma=False)
```

```python
import functools

import jax
import jax.numpy as jnp
from jax import lax
from jax.experimental import pallas as pl
from jax.experimental.pallas import tpu as pltpu
from jax.sharding import PartitionSpec as P

F32 = jnp.float32
BF16 = jnp.bfloat16
VMEM = 44 * 2**20


def block(total, limit):
    best = 128
    for width in range(128, min(total, limit) + 1, 128):
        if total % width == 0:
            best = width
    return best


def launch(kernel, grid, in_specs, out_specs, out_shape, args, after=(), carry=(), scratch=(), flops=0, vmem=VMEM, name="kernel"):
    many = isinstance(out_shape, list)
    shapes = out_shape if many else [out_shape]
    specs = out_specs if many else [out_specs]
    hidden = len(after) + len(carry)
    idle = [pl.BlockSpec(memory_space=pl.ANY)]

    def wrapped(*refs):
        inputs, rest = refs[: len(args)], refs[len(args) + hidden :]
        kernel(*inputs, *rest[: len(shapes)], *rest[len(shapes) + len(carry) :])

    results = pl.pallas_call(
        wrapped,
        grid=grid,
        in_specs=list(in_specs) + idle * hidden,
        out_specs=specs + idle * len(carry),
        out_shape=shapes + [jax.ShapeDtypeStruct(c.shape, c.dtype) for c in carry],
        input_output_aliases={len(args) + len(after) + n: len(shapes) + n for n in range(len(carry))},
        scratch_shapes=list(scratch),
        compiler_params=pltpu.CompilerParams(vmem_limit_bytes=vmem),
        cost_estimate=pl.CostEstimate(flops=int(flops), bytes_accessed=int(flops / 300), transcendentals=0),
        name=name,
    )(*args, *after, *carry)
    own = results[: len(shapes)]
    return (list(own) if many else own[0]), list(results[len(shapes) :])


def project(rows, weight, dim, halves=1, after=(), carry=(), limit=1536):
    count, depth = rows.shape
    width = weight.shape[1 - dim]
    step = block(width, limit)
    part_rows = count // halves

    def kernel(x, w, *outs):
        dims = (((1,), (dim,)), ((), ()))
        part = lax.dot_general(x[...], w[...], dims, preferred_element_type=F32).astype(BF16)
        for n, o in enumerate(outs):
            o[...] = part[n * part_rows : (n + 1) * part_rows]

    spec = pl.BlockSpec((depth, step), lambda i: (0, i)) if dim == 0 else pl.BlockSpec((step, depth), lambda i: (i, 0))
    return launch(
        kernel,
        (width // step,),
        [pl.BlockSpec((count, depth), lambda i: (0, 0)), spec],
        [pl.BlockSpec((part_rows, step), lambda i: (0, i))] * halves,
        [jax.ShapeDtypeStruct((part_rows, width), BF16)] * halves,
        (rows, weight),
        after,
        carry,
        flops=4 * count * depth * width,
        vmem=58 * 2**20,
        name="project",
    )


def parts_specs(parts, which, step, index):
    blocks, _, rows, _ = parts[0].shape
    return [pl.BlockSpec((blocks, 1, rows, step), lambda i: (0, which, 0, index(i)))] * len(parts)


def whole_rows(refs):
    blocks, _, rows, step = refs[0].shape
    whole = [r[:, 0].reshape(blocks * rows, step) for r in refs]
    return whole[0] if len(whole) == 1 else jnp.concatenate(whole)


def consume(parts, side, weight, dim, hidden_rows, after=(), carry=(), limit=1536):
    count, depth = side.shape if hidden_rows else side.shape[::-1]
    width = parts[0].shape[3]
    step = block(width, limit)

    def fold(squares):
        folded = squares[:, :128]
        for j in range(1, squares.shape[1] // 128):
            folded += squares[:, j * 128 : (j + 1) * 128]
        return folded

    def kernel(x, w, *rest):
        grad, cols, feature, product, sums, total = rest[-6:]
        i = pl.program_id(0)
        a = whole_rows(rest[:-6])
        here = pl.ds(pl.multiple_of(i * step, step), step)
        if hidden_rows:
            g = lax.dot_general(a, x[...], (((0,), (0,)), ((), ())), preferred_element_type=F32)
            grad[here, :] = g.astype(BF16)
            s = g * g
            cols[...] = jnp.sum(jnp.transpose(fold(s)), axis=0, keepdims=True)
            across = jnp.broadcast_to(jnp.sum(s, axis=0, keepdims=True), (8, depth))
        else:
            g = jnp.dot(x[...], a, preferred_element_type=F32)
            grad[:, here] = g.astype(BF16)
            s = g * g
            cols[...] = jnp.sum(s, axis=0, keepdims=True)
            across = fold(s)
        part = lax.dot_general(a, w[...], (((1,), (dim,)), ((), ())), preferred_element_type=F32)

        @pl.when(i == 0)
        def _():
            sums[...] = across
            total[...] = part

        @pl.when(i != 0)
        def _():
            sums[...] += across
            total[...] += part

        @pl.when(i == width // step - 1)
        def _():
            row = sums[:1, :] if hidden_rows else jnp.sum(jnp.transpose(sums[...]), axis=0, keepdims=True)
            feature[:, :depth] = jnp.broadcast_to(row, (8, depth))
            feature[:, depth:] = jnp.broadcast_to(jnp.sum(row, axis=1, keepdims=True), (8, 128))
            product[...] = total[...].astype(BF16)

    spec = pl.BlockSpec((step, depth), lambda i: (i, 0)) if dim == 0 else pl.BlockSpec((depth, step), lambda i: (0, i))
    return launch(
        kernel,
        (width // step,),
        [pl.BlockSpec(side.shape, lambda i: (0, 0)), spec] + parts_specs(parts, 0, step, lambda i: i),
        [
            pl.BlockSpec(memory_space=pltpu.VMEM),
            pl.BlockSpec((1, step), lambda i: (0, i)),
            pl.BlockSpec((8, depth + 128), lambda i: (0, 0)),
            pl.BlockSpec((count, depth), lambda i: (0, 0)),
        ],
        [
            pltpu.VMEM((width, depth) if hidden_rows else (depth, width), BF16),
            jax.ShapeDtypeStruct((1, width), F32),
            jax.ShapeDtypeStruct((8, depth + 128), F32),
            jax.ShapeDtypeStruct((count, depth), BF16),
        ],
        (side, weight, *parts),
        after,
        carry,
        scratch=[pltpu.VMEM((8, depth) if hidden_rows else (depth, 128), F32), pltpu.VMEM((count, depth), F32)],
        flops=8 * count * depth * width,
        name="consume",
    )


def gelu(pre):
    phi = 0.5 * (1.0 + lax.erf(pre * 0.7071067811865476))
    slope = phi + pre * jnp.exp(-0.5 * pre * pre) * 0.3989422804014327
    return pre * phi, slope


def activate(pre, grad, after=(), carry=()):
    rows, width = pre.shape
    step = block(width, 3072)

    def kernel(p, g, hidden, act):
        value, slope = gelu(p[...].astype(F32))
        hidden[0] = value.astype(BF16)
        act[0] = (g[...].astype(F32) * slope).astype(BF16)

    spec = pl.BlockSpec((rows, step), lambda i: (0, i))
    return launch(
        kernel,
        (width // step,),
        [spec, spec],
        [pl.BlockSpec((1, rows, step), lambda i: (0, 0, i))] * 2,
        [jax.ShapeDtypeStruct((1, rows, width), BF16)] * 2,
        (pre, grad),
        after,
        carry,
        flops=1e9,
        vmem=58 * 2**20,
        name="activate",
    )


def add_partials(first, second, after=(), carry=()):
    rows, width = first.shape
    step = block(width, 1536)

    def kernel(a, b, o):
        o[...] = (a[...].astype(F32) + b[...].astype(F32)).astype(BF16)

    spec = pl.BlockSpec((rows, step), lambda i: (0, i))
    return launch(
        kernel,
        (width // step,),
        [spec, spec],
        spec,
        jax.ShapeDtypeStruct((rows, width), BF16),
        (first, second),
        after,
        carry,
        flops=1e9,
        vmem=58 * 2**20,
        name="add_partials",
    )


def settle(after, carry):
    return launch(lambda: None, (1,), [], [], [], (), after, carry, vmem=60 * 2**20, name="settle")


def write_update(grad, feature_sum, hidden_sums, before, sizes, hidden_rows, after=(), carry=(), limit=1536):
    total, features = grad.shape if hidden_rows else grad.shape[::-1]
    step = block(total, limit)
    model, hidden_units = sizes

    def tall(row):
        return jnp.transpose(jnp.broadcast_to(row, (8, row.shape[1])))[:, :1]

    def kernel(whole, across, near_sum, far_sum, near_all, far_all, feature_before, hidden_before, mean_before, o):
        here = pl.ds(pl.multiple_of(pl.program_id(0) * step, step), step)
        g = (whole[here, :] if hidden_rows else whole[:, here]).astype(F32)
        grand = (near_all[:, :1] + far_all[:, :1]) / model / hidden_units + 1e-30
        mean = 0.9 * mean_before[:, :1] + 0.1 * grand
        by_feature = 0.9 * feature_before[...] + 0.1 * (across[:1, :features] / hidden_units + 1e-30)
        by_hidden = 0.9 * hidden_before[...] + 0.1 * ((near_sum[...] + far_sum[...]) / model + 1e-30)
        by_feature = lax.rsqrt(by_feature) * jnp.sqrt(mean)
        by_hidden = lax.rsqrt(by_hidden)
        if hidden_rows:
            o[...] = g * tall(by_hidden) * by_feature
        else:
            o[...] = g * tall(by_feature) * by_hidden

    along_hidden = pl.BlockSpec((1, step), lambda i: (0, i))
    behind = pl.BlockSpec((1, 128), lambda i: (0, total // 128))
    scale_specs = [
        pl.BlockSpec((8, features + 128), lambda i: (0, 0)),
        along_hidden,
        along_hidden,
        behind,
        behind,
        pl.BlockSpec((1, features), lambda i: (0, 0)),
        along_hidden,
        pl.BlockSpec((1, 128), lambda i: (0, 0)),
    ]
    if hidden_rows:
        out_spec = pl.BlockSpec((step, features), lambda i: (i, 0))
        shape = (total, features)
    else:
        out_spec = pl.BlockSpec((features, step), lambda i: (0, i))
        shape = (features, total)
    return launch(
        kernel,
        (total // step,),
        [pl.BlockSpec(memory_space=pltpu.VMEM)] + scale_specs,
        out_spec,
        jax.ShapeDtypeStruct(shape, F32),
        (grad, feature_sum, *hidden_sums, *hidden_sums, *before),
        after,
        carry,
        flops=1500 * features * total,
        name="write_update",
    )


def power_of_two(size):
    return size & (size - 1) == 0


def all_sum(value, axis, split=False):
    size = lax.axis_size(axis)
    if not power_of_two(size):
        value = lax.psum(value, axis)
        return (value, jnp.zeros_like(value)) if split else value
    bit = 1
    while bit < size:
        count = min(4, size // bit)
        arrived = [lax.ppermute(value, axis, [(i, i ^ (bit * n)) for i in range(size)]) for n in range(1, count)]
        bit *= count
        if split and bit >= size:
            return functools.reduce(jnp.add, arrived[1:], value), arrived[0]
        value = functools.reduce(jnp.add, arrived, value)
    return (value, jnp.zeros_like(value)) if split else value


def gather_rows(share, axis):
    size = lax.axis_size(axis)
    if not power_of_two(size):
        return lax.all_gather(share, axis, axis=0, tiled=True)
    blocks = [share]
    for bits in range(1, size):
        blocks.append(lax.ppermute(share, axis, [(i, i ^ bits) for i in range(size)]))
    return jnp.concatenate(blocks)


def scatter_rows(partial, axis):
    size = lax.axis_size(axis)
    if not power_of_two(size):
        return lax.psum_scatter(partial, axis, scatter_dimension=0, tiled=True).astype(F32)
    share = partial.shape[0] // size
    total = partial[:share].astype(F32)
    for bits in range(1, size):
        part = partial[bits * share : (bits + 1) * share]
        total = total + lax.ppermute(part, axis, [(i, i ^ bits) for i in range(size)]).astype(F32)
    return total


def body(patches, ln_gain, weight_in, weight_out, upstream, row_in, col_in, row_out, col_out):
    gx, gy = lax.axis_size("gx"), lax.axis_size("gy")
    width = weight_in.shape[1]
    features = patches.shape[1]
    model, hidden_units = features * gx, width * gy

    core = lax.axis_index("gx") % 2

    state = [lax.axis_index("gx").astype(jnp.int32)[None]]

    def run(function, *args, **kwargs):
        results, carried = function(*args, carry=[state[0]], **kwargs)
        state[0] = carried[0]
        return results

    def share_sum(partial):
        return lax.psum_scatter(partial, "gx", scatter_dimension=0, tiled=True)

    up_full = gather_rows(upstream, "gy")
    x_float = patches.astype(F32)
    stats = all_sum(jnp.stack([jnp.sum(x_float, axis=1), jnp.sum(x_float * x_float, axis=1)]), "gx") / model
    row_mean = stats[0][:, None]
    inv_std = lax.rsqrt(stats[1][:, None] - row_mean * row_mean + 1e-06)
    unit = (x_float - row_mean) * inv_std
    normed = (unit * ln_gain[None, :]).astype(BF16)
    normed_full = gather_rows(normed, "gy")

    (grad,) = run(project, up_full, weight_out, 1)
    grad = share_sum(grad)

    own = lax.dynamic_index_in_dim(normed_full.reshape(gx // 2, 2, -1, features), core, 1, keepdims=False)
    other = lax.dynamic_index_in_dim(normed_full.reshape(gx // 2, 2, -1, features), 1 - core, 1, keepdims=False)
    halves = jnp.concatenate([own, other]).reshape(normed_full.shape)
    pre_own, pre_other = run(project, halves, weight_in, 0, 2)
    pre_other = lax.ppermute(pre_other, "gx", [(i, i ^ 1) for i in range(gx)])
    both = run(add_partials, pre_own, pre_other)
    (both,) = settle([grad], [both])[1]
    pre = lax.psum_scatter(
        both,
        "gx",
        scatter_dimension=0,
        axis_index_groups=[list(range(c, gx, 2)) for c in (0, 1)],
        tiled=True,
    )
    normed_side = normed_full.T

    def all_rows(share):
        return [lax.all_gather(share, "gx", axis=0)]

    hidden, act = run(activate, pre, grad)
    act_parts, hidden_parts = all_rows(act), all_rows(hidden)

    def mean_of(factor, axis):
        return jnp.full((1, 128), all_sum(jnp.full((128,), jnp.sum(factor)), axis)[0] / (factor.shape[0] * lax.axis_size(axis)))

    mean_in, mean_out = mean_of(row_in, "gx"), mean_of(row_out, "gy")
    sizes = (float(model), float(hidden_units))

    grad_in, hidden_sum, feature_sum, normed_grad = run(
        consume, act_parts, normed_side, weight_in, 1, False, after=[mean_in, mean_out]
    )
    feature_sum = all_sum(feature_sum, "gy")
    scaled = scatter_rows(normed_grad, "gy") * ln_gain[None, :]
    norm_sums = jnp.concatenate([jnp.sum(scaled, axis=1), jnp.sum(scaled * unit, axis=1)])[None, :]
    hidden_sum = jnp.concatenate([hidden_sum, feature_sum[:1, features:], norm_sums], axis=1)
    hidden_sums = all_sum(hidden_sum, "gx", True)
    means = (hidden_sums[0] + hidden_sums[1])[0, width + 128 :].reshape(2, -1, 1) / model
    input_grad = upstream.astype(F32) + inv_std * (scaled - means[0] - unit * means[1])
    before = (row_in[None, :], col_in[None, :], mean_in)
    update_in = run(write_update, grad_in, feature_sum, hidden_sums, before, sizes, False, after=[input_grad])

    grad_out, hidden_sum, feature_sum, branch = run(consume, hidden_parts, up_full, weight_out, 0, True)
    feature_sum = all_sum(feature_sum, "gy")
    hidden_sums = all_sum(jnp.concatenate([hidden_sum, feature_sum[:1, features:]], axis=1), "gx", True)
    before = (col_out[None, :], row_out[None, :], mean_out)
    update_out = run(write_update, grad_out, feature_sum, hidden_sums, before, sizes, True)
    output = (x_float + scatter_rows(branch, "gy")).astype(BF16)
    return (output, input_grad, update_in, update_out)


def solution(mesh):
    in_specs = (
        P("gy", "gx"),
        P("gx"),
        P("gx", "gy"),
        P("gy", "gx"),
        P("gy", "gx"),
        P("gx"),
        P("gy"),
        P("gy"),
        P("gx"),
    )
    out_specs = (P("gy", "gx"), P("gy", "gx"), P("gx", "gy"), P("gy", "gx"))
    return jax.shard_map(body, mesh=mesh, in_specs=in_specs, out_specs=out_specs, check_vma=False)
```
